512 devices in a mesh: dp: 4 (over x), expert: 128 (over z, y, core).
Axes of the slice: x: 4, y: 8, z: 8, core: 2. Of those that a mesh axis runs over, the one named last changes fastest.
Arguments:
- residual: bfloat16 [32768, 1024], P(('dp', 'expert')), parts along dimension 0, may hold values from -6 to 6
- expert_ids: int32 [32768, 8], P(('dp', 'expert')), parts along dimension 0, may hold values from 0 to 63, all different within a row; in each aligned block of 64 rows (0 to 63, 64 to 127, ...) at most 12 rows name the same one
- route_weights: float32 [32768, 8], P(('dp', 'expert')), parts along dimension 0, may hold values from 0.05 to 0.5
- expert_out: bfloat16 [393216, 1024], P(('dp', 'expert')), parts along dimension 0, may hold values from -6 to 6
Outputs:
- mixed: bfloat16 [32768, 1024], P(('dp', 'expert')), parts along dimension 0
- expert_load: float32 [256], P('dp'), parts along dimension 0
The draws below stay inside these ranges and needn't reach their ends.
There are 4 independent parts, one for each index of `dp`. The reference program is written for one: setup_inputs(seed, part) draws one part's arguments, and reference() takes and returns one part's arrays. A program takes and returns all parts, laid end to end along the dimension named above; each array names one. Nothing has to cross between parts.
Inputs may be any that keep to these rules, and one draw needn't show every extreme that they name: `expert_ids`: each row names 8 different experts. Within the rows of one device no expert is named by more than 12 rows, and in some devices' rows an expert is named by exactly 12.
All inputs are finite; a program needn't handle non-finite values.
Results may differ from the reference program's by a relative error of at most 0.001.
Values may be sent and summed in bfloat16 or wider, within the bound.
No kernel may reach another device: no remote copies, remote signals or barrier semaphores. Data moves between devices by JAX's collectives and lax.ppermute only.
A program may use at most 64 MiB of HBM per device.

```python
import math
import jax
import jax.numpy as jnp
import numpy as np
from jax import lax

D = 1024
EXPERTS = 64
TOP = 8
TOK_DEV = 64
CAP_E = 12
TOKENS = 8192
SLOT_ROWS = 98304
N_EXPERT = 128


def steps_of(key, shape, shards, smallest, top_value):
    def one(dim, shards_of):
        heights = jax.random.uniform(jax.random.fold_in(jax.random.fold_in(key, 6), dim), (shards_of,), jnp.float32, smallest / len(shards), top_value / len(shards))
        return jnp.repeat(jnp.exp(heights), shape[dim] // shards_of).reshape((-1,) + (1,) * (len(shape) - dim - 1))

    loudness = one(*shards[0])
    for cut in shards[1:]:
        loudness = loudness * one(*cut)
    return loudness


def shared_out(stream_key, own, number, rows, count, top, bound, slope):
    sequence = jax.random.permutation(stream_key, count)
    packed, ordinary = portions_of(count, rows * top, bound, slope, True), portions_of(count, rows * top, bound, slope, False)
    places = jnp.arange(count)

    def named(tallies, turn):
        used = int((tallies > 0).sum())
        fixed = max(1, used // 4)
        moved = fixed + (places - fixed + turn * (used - fixed)) % max(1, count - fixed)
        return jnp.zeros((count,), jnp.int32).at[sequence[jnp.where(places < fixed, places, moved)]].set(jnp.asarray(tallies, jnp.int32))

    tallies = jnp.where(number % 4 == 0, named(packed, number // 4), named(ordinary, number - number // 4 - 1))
    mixed = jax.random.permutation(jax.random.fold_in(own, 3), count)
    donor, taker = mixed[0:count // 2 * 2:2], mixed[1:count // 2 * 2:2]
    room = jnp.minimum(tallies[donor] - 1, bound - tallies[taker]) // 2
    room = jnp.where((donor == sequence[0]) | (taker == sequence[0]) | (tallies[taker] == 0), 0, jnp.maximum(room, 0))
    moved = jax.random.randint(jax.random.fold_in(own, 4), (count // 2,), 0, 1 << 20) % (room + 1)
    tallies = tallies.at[donor].add(-moved).at[taker].add(moved)
    members = jnp.searchsorted(jnp.cumsum(tallies), jnp.arange(rows * top), side="right").astype(jnp.int32)
    table = members.reshape(top, rows).T
    table = table[jax.random.permutation(jax.random.fold_in(own, 1), rows)]
    turn = jax.random.randint(jax.random.fold_in(own, 2), (rows, 1), 0, top)
    return jnp.take_along_axis(table, (jnp.arange(top)[None, :] + turn) % top, axis=1)


def portions_of(amount, total, most, slope, full):
    weights = [(1 << 20) // math.isqrt(rank ** slope) + 1 for rank in range(1, amount + 1)]
    largest = most if full else min(most, max(-(-total // amount), total * weights[0] // sum(weights)))
    least = 1 if total - largest >= amount - 1 else 0
    counts, spare = [largest] + [least] * (amount - 1), total - largest - least * (amount - 1)
    while spare > 0:
        candidates = [i for i in range(1, amount) if counts[i] < largest] or [i for i in range(1, amount) if counts[i] < most]
        pool, left = sum([weights[i] for i in candidates]), spare
        for i in candidates:
            addition = min(most - counts[i], max(1, left * weights[i] // pool), spare)
            counts[i] = counts[i] + addition
            spare = spare - addition
    return np.array(counts)


def bell_draw(stream_key, shape, scale, most, split=(), kind=jnp.bfloat16):
    entries = jax.random.normal(stream_key, shape, jnp.float32) * scale
    if len(split) > 0:
        entries = steps_of(stream_key, shape, split, -0.22, 0.18) * entries
    return jnp.clip(entries, min=-most, max=most).astype(kind)


def setup_inputs(seed: int = 0, part: int = 0) -> dict:
    streams_of = jax.random.split(jax.random.key(seed), 5)
    part_splits = jax.random.split(jax.random.fold_in(streams_of[4], part), 5)
    residual = bell_draw(part_splits[0], (TOKENS, D), 1.0, 6.0, ((0, 128),))
    expert_ids_keys = jax.random.split(jax.random.fold_in(part_splits[1], 1), TOKENS // TOK_DEV)
    expert_ids_turns = jax.random.permutation(jax.random.fold_in(part_splits[1], 3), TOKENS // TOK_DEV)
    expert_ids = jax.vmap(lambda own, number: shared_out(jax.random.fold_in(part_splits[1], 2), own, number, TOK_DEV, EXPERTS, TOP, CAP_E, 2))(expert_ids_keys, expert_ids_turns).reshape((TOKENS, TOP))
    route_weights = jnp.clip(jnp.exp(math.log(0.5) - 2.3025851 * jax.random.uniform(part_splits[2], (TOKENS, TOP), jnp.float32) ** steps_of(part_splits[2], (TOKENS, TOP), ((0, 128),), -0.2, 0.2)), 0.05, 0.5)
    expert_out = bell_draw(part_splits[3], (SLOT_ROWS, D), 1.0, 6.0, ((0, 128),))
    return {"residual": residual, "expert_ids": expert_ids, "route_weights": route_weights, "expert_out": expert_out}


def reference(residual, expert_ids, route_weights, expert_out):
    per_peer = EXPERTS * CAP_E // N_EXPERT
    held_rows = EXPERTS * CAP_E
    catalog = jnp.arange(EXPERTS, dtype=jnp.int32)

    def one_owner(owner):
        routes = lax.dynamic_slice_in_dim(expert_ids, owner * TOK_DEV, TOK_DEV, 0).reshape(-1)
        onehot = (routes[:, None] == catalog[None, :]).astype(jnp.int32)
        earlier = jnp.cumsum(onehot, axis=0, dtype=jnp.int32) - onehot
        slots = jnp.sum(earlier * onehot, axis=1, dtype=jnp.int32)
        position = routes * CAP_E + slots
        rows = (position // per_peer) * held_rows + owner * per_peer + position % per_peer
        picked = jnp.take(expert_out, rows.astype(jnp.int32), axis=0).reshape(TOK_DEV, TOP, D)
        weights = lax.dynamic_slice_in_dim(route_weights, owner * TOK_DEV, TOK_DEV, 0)
        total = lax.dynamic_slice_in_dim(residual, owner * TOK_DEV, TOK_DEV, 0).astype(jnp.float32)
        for choice_index in range(TOP):
            total = total + weights[:, choice_index:choice_index + 1] * picked[:, choice_index].astype(jnp.float32)
        return total.astype(jnp.bfloat16), jnp.sum(onehot, axis=0, dtype=jnp.int32)

    mixed, loads = lax.map(one_owner, jnp.arange(N_EXPERT, dtype=jnp.int32))
    return mixed.reshape(TOKENS, D), jnp.sum(loads, axis=0, dtype=jnp.int32).astype(jnp.float32)
```

```python
import jax
import jax.numpy as jnp
from jax import lax
from jax.experimental import pallas as pl
from jax.experimental.pallas import tpu as pltpu
from jax.sharding import PartitionSpec as P

EXPERTS = 64
TOP = 8
TOK = 64
HELD = 6
PEERS = 128
COLS = 256
UNITS = 3
GROUP = 16
VMEM = 24 * 2**20


def iota(shape, dim):
    return lax.broadcasted_iota(jnp.int32, shape, dim)


def pack_kernel(x_hbm, ids_hbm, out_ref, counts_ref, x_ref, ids_ref, x_sems, ids_sem):
    rows = GROUP * HELD
    groups = PEERS // GROUP
    x_copies = [
        pltpu.make_async_copy(
            x_hbm.at[pl.ds(g * rows, rows)], x_ref.at[pl.ds(g * rows, rows)], x_sems.at[g]
        )
        for g in range(groups)
    ]
    ids_copy = pltpu.make_async_copy(ids_hbm, ids_ref, ids_sem)
    ids_copy.start()
    for copy in x_copies:
        copy.start()
    line, column = iota((GROUP * 8, 2 * rows), 0), iota((GROUP * 8, 2 * rows), 1)
    owner, r = GROUP - 1 - line // 8, line % 8
    pick = []
    for u in range(UNITS):
        wanted = jnp.where(r < HELD, HELD * owner + r, rows + HELD * owner + 2 * u + r - HELD)
        pick.append((column == wanted).astype(jnp.float32).astype(jnp.bfloat16))
    ids_copy.wait()
    expert = iota((EXPERTS, TOK), 0)
    named = jnp.zeros((EXPERTS, TOK), jnp.float32)
    for k in range(TOP):
        named = named + (ids_ref[k : k + 1, :] == expert).astype(jnp.float32)
    counts_ref[...] = lax.dot_general(
        jnp.ones((8, TOK), jnp.bfloat16),
        named.astype(jnp.bfloat16),
        (((1,), (1,)), ((), ())),
        preferred_element_type=jnp.float32,
    )
    for g in range(groups):
        x_copies[g].wait()
        here = pl.ds(g * rows, rows)
        last = x_ref[here, UNITS * COLS :]
        for u in range(UNITS):
            source = jnp.concatenate([x_ref[here, u * COLS : (u + 1) * COLS], last], axis=0)
            packed = jnp.dot(pick[u], source, preferred_element_type=jnp.float32)
            out_ref[pl.ds((groups - 1 - g) * GROUP, GROUP), u] = packed.astype(
                jnp.bfloat16
            ).reshape(GROUP, 8, COLS)


def weights_kernel(ids_ref, route_ref, out_ref):
    expert = iota((EXPERTS, TOK), 0)
    named = jnp.zeros((EXPERTS, TOK), jnp.float32)
    weight = jnp.zeros((EXPERTS, TOK), jnp.float32)
    for k in range(TOP):
        hit = ids_ref[k : k + 1, :] == expert
        named = jnp.where(hit, 1.0, named)
        weight = jnp.where(hit, route_ref[k : k + 1, :], weight)
    before = (iota((TOK, TOK), 0) < iota((TOK, TOK), 1)).astype(jnp.float32)
    slot = jnp.dot(
        named.astype(jnp.bfloat16), before.astype(jnp.bfloat16), preferred_element_type=jnp.float32
    )
    slot = jnp.where(named > 0, slot, -1.0)
    high = weight.astype(jnp.bfloat16)
    low = (weight - high.astype(jnp.float32)).astype(jnp.bfloat16)
    lines = 8 * PEERS
    lane = iota((EXPERTS, lines), 1)
    holder = PEERS - 1 - lane // 8
    spread = (holder // 2 == iota((EXPERTS, lines), 0)).astype(jnp.float32).astype(jnp.bfloat16)

    def over_lines(table):
        return lax.dot_general(
            table, spread, (((0,), (0,)), ((), ())), preferred_element_type=jnp.float32
        )

    slots = over_lines(slot.astype(jnp.bfloat16))
    highs, lows = over_lines(high), over_lines(low)
    lane = iota((TOK, lines), 1)
    first, r = HELD * ((PEERS - 1 - lane // 8) % 2), lane % 8
    main = slots == jnp.where(r < HELD, first + r, -2).astype(jnp.float32)
    for u in range(UNITS):
        rest = slots == jnp.where(r < HELD, -2, first + 2 * u + r - HELD).astype(jnp.float32)
        for i, (hit, part) in enumerate(((main, highs), (main, lows), (rest, highs), (rest, lows))):
            out_ref[u, i * TOK : (i + 1) * TOK, :] = jnp.where(hit, part, 0.0).astype(jnp.bfloat16)


def combine_kernel(weights_ref, arrived_ref, residual_ref, out_ref):
    last = residual_ref[:, UNITS * COLS :].astype(jnp.float32)
    for u in range(UNITS):
        lines = arrived_ref[:, u].reshape(8 * PEERS, COLS)
        sums = jnp.dot(weights_ref[u], lines, preferred_element_type=jnp.float32)
        here = slice(u * COLS, (u + 1) * COLS)
        out_ref[:, here] = (
            residual_ref[:, here].astype(jnp.float32) + (sums[:TOK] + sums[TOK : 2 * TOK])
        ).astype(jnp.bfloat16)
        last = last + (sums[2 * TOK : 3 * TOK] + sums[3 * TOK :])
    out_ref[:, UNITS * COLS :] = last.astype(jnp.bfloat16)


def per_device(residual, expert_ids, route_weights, expert_out):
    width = expert_out.shape[1]
    ids, routes = expert_ids.T, route_weights.T
    in_vmem = pl.BlockSpec(memory_space=pltpu.VMEM)
    anywhere = pl.BlockSpec(memory_space=pl.ANY)
    rows = GROUP * HELD
    packed, counts = pl.pallas_call(
        pack_kernel,
        out_shape=(
            jax.ShapeDtypeStruct((PEERS, UNITS, 8, COLS), jnp.bfloat16),
            jax.ShapeDtypeStruct((8, EXPERTS), jnp.float32),
        ),
        in_specs=[anywhere, anywhere],
        out_specs=(in_vmem, in_vmem),
        scratch_shapes=[
            pltpu.VMEM(expert_out.shape, jnp.bfloat16),
            pltpu.VMEM(ids.shape, jnp.int32),
            pltpu.SemaphoreType.DMA((PEERS // GROUP,)),
            pltpu.SemaphoreType.DMA,
        ],
        compiler_params=pltpu.CompilerParams(vmem_limit_bytes=VMEM),
        name="pack",
    )(expert_out, ids)
    along_z = [[z * 16 + i for z in range(8)] for i in range(16)]
    plane = [[z * 16 + i for i in range(16)] for z in range(8)]
    gathered = lax.all_gather(counts[:1], "expert", axis=0, axis_index_groups=along_z, tiled=True)
    gathered = lax.all_gather(
        jnp.sum(gathered, axis=0, keepdims=True),
        "expert",
        axis=0,
        axis_index_groups=plane,
        tiled=True,
    )
    load = jnp.sum(gathered, axis=0)
    arrived = lax.all_to_all(
        packed.reshape(PEERS, UNITS * 8, COLS),
        "expert",
        split_axis=0,
        concat_axis=0,
        axis_index_groups=[list(range(PEERS - 1, -1, -1))],
        tiled=True,
    ).reshape(PEERS, UNITS, 8, COLS)
    weights = pl.pallas_call(
        weights_kernel,
        out_shape=jax.ShapeDtypeStruct((UNITS, 4 * TOK, 8 * PEERS), jnp.bfloat16),
        in_specs=[in_vmem, in_vmem],
        out_specs=in_vmem,
        compiler_params=pltpu.CompilerParams(vmem_limit_bytes=VMEM),
        name="weights",
    )(ids, routes)
    mixed = pl.pallas_call(
        combine_kernel,
        out_shape=jax.ShapeDtypeStruct((TOK, width), jnp.bfloat16),
        in_specs=[in_vmem, in_vmem, in_vmem],
        out_specs=in_vmem,
        compiler_params=pltpu.CompilerParams(vmem_limit_bytes=VMEM),
        name="combine",
    )(weights, arrived, residual)
    return mixed, load


def solution(mesh):
    placed = P(("dp", "expert"), None)
    return jax.shard_map(
        per_device,
        mesh=mesh,
        in_specs=(placed, placed, placed, placed),
        out_specs=(placed, P("dp")),
        check_vma=False,
    )
```

```python
import jax
import jax.numpy as jnp
from jax import lax
from jax.experimental import pallas as pl
from jax.experimental.pallas import tpu as pltpu
from jax.sharding import PartitionSpec as P

EXPERTS = 64
TOP = 8
TOK = 64
HELD = 6
PEERS = 128
LANES = 128
LINES = 50
QUAD = 4
TILES = QUAD * LINES // 8
OCT = 8
DATA = OCT * HELD * 8

FIRST = (0, 6, 13, 19)


def iota(shape, dim):
    return lax.broadcasted_iota(jnp.int32, shape, dim)


def as_bf16(mask):
    return mask.astype(jnp.float32).astype(jnp.bfloat16)


def pack_kernel(x_hbm, ids_hbm, out_hbm, x_ref, ids_ref, out_ref, x_sems, ids_sem, out_sems):
    rows = 2 * OCT * HELD
    steps = PEERS // (2 * OCT)
    x_copies, out_copies = [], []
    for g in range(steps):
        here = pl.ds(g * rows, rows)
        there = pl.ds((steps - 1 - g) * 2 * OCT * LINES, 2 * OCT * LINES)
        x_copies.append(pltpu.make_async_copy(x_hbm.at[here], x_ref.at[here], x_sems.at[g]))
        out_copies.append(
            pltpu.make_async_copy(out_ref.at[there], out_hbm.at[there], out_sems.at[g])
        )
    ids_copy = pltpu.make_async_copy(ids_hbm, ids_ref, ids_sem)
    ids_copy.start()
    for copy in x_copies:
        copy.start()
    block = (PEERS - 1 - lax.axis_index("expert")) % QUAD
    line = iota((OCT * LINES, LANES), 0)
    owner = line * 0
    for b in range(1, OCT):
        owner = jnp.where(line >= b * LINES, b, owner)
    place = line - owner * LINES + block * LINES
    t, r = place >> 3, place & 7
    c = t - jnp.where(t < 6, 0, jnp.where(t < 12, 6, jnp.where(t < 19, 13, 19)))
    main = jnp.where(t == 6, r - 2, r)
    rest = jnp.where(t == 12, jnp.where(r < 2, 0, 5), c)
    rest_row = 2 * jnp.where(rest >= 3, rest - 3, rest) + jnp.where(r < 2, r, r - 6)
    source = jnp.where((t != 12) & (main >= 0) & (main < HELD), OCT * HELD * c + main, 0)
    is_rest = ((t == 12) & (r < 2)) | ((t != 6) & (t != 18) & (r >= 6))
    source = jnp.where(
        is_rest, OCT * HELD * jnp.where(rest >= 3, 7, 6) + rest_row, source
    )
    source = source + HELD * (OCT - 1 - owner)
    tally = ((t == 6) & (r < 2)) | ((t == 12) & (r >= 2) & (r < 6)) | ((t == 18) & (r >= 6))
    source = jnp.where(tally, jnp.where((r & 1) == 0, DATA, -1), source)
    column = iota((OCT * LINES, LANES), 1)
    tails = (LANES, LANES, LANES, 16)
    pick = jnp.concatenate(
        [as_bf16(source == column + i * LANES)[:, :n] for i, n in enumerate(tails)], axis=1
    )
    ids_copy.wait()
    expert = iota((LANES, TOK), 0)
    named = jnp.zeros((LANES, TOK), jnp.float32)
    for k in range(TOP):
        named = named + (ids_ref[k : k + 1, :] == expert).astype(jnp.float32)
    counts = lax.dot_general(
        jnp.ones((16, TOK), jnp.bfloat16),
        named.astype(jnp.bfloat16),
        (((1,), (1,)), ((), ())),
        preferred_element_type=jnp.float32,
    ).astype(jnp.bfloat16)
    counts = jnp.concatenate([counts, counts], axis=1)
    for copy in x_copies:
        copy.wait()
    for g in range(steps):
        one = x_ref[pl.ds(g * rows, rows // 2), :]
        two = x_ref[pl.ds(g * rows + rows // 2, rows // 2), :]
        stack = [
            jnp.concatenate(
                [one[:, i * LANES : (i + 1) * LANES], two[:, i * LANES : (i + 1) * LANES]], axis=1
            )
            for i in range(8)
        ]
        packed = jnp.dot(
            pick, jnp.concatenate(stack + [counts], axis=0), preferred_element_type=jnp.float32
        ).astype(jnp.bfloat16)
        start = (steps - 1 - g) * 2 * OCT * LINES
        out_ref[pl.ds(start + OCT * LINES, OCT * LINES), :] = packed[:, :LANES]
        out_ref[pl.ds(start, OCT * LINES), :] = packed[:, LANES:]
        if g % 2:
            out_copies[g - 1].start()
            out_copies[g].start()
    for copy in out_copies:
        copy.wait()


def weights_kernel(ids_ref, route_ref, out_ref, odd_ref):
    expert = iota((EXPERTS, TOK), 0)
    named = jnp.zeros((EXPERTS, TOK), jnp.float32)
    weight = jnp.zeros((EXPERTS, TOK), jnp.float32)
    for k in range(TOP):
        hit = ids_ref[k : k + 1, :] == expert
        named = jnp.where(hit, 1.0, named)
        weight = jnp.where(hit, route_ref[k : k + 1, :], weight)
    before = as_bf16(iota((TOK, TOK), 0) < iota((TOK, TOK), 1))
    slot = jnp.dot(named.astype(jnp.bfloat16), before, preferred_element_type=jnp.float32)
    slot = jnp.where(named > 0, slot, -1.0)
    high = weight.astype(jnp.bfloat16)
    low = (weight - high.astype(jnp.float32)).astype(jnp.bfloat16)
    width = 8 * PEERS
    per_block = width // QUAD

    def holder_of(line):
        return PEERS - 1 - (QUAD * ((line % per_block) // 8) + line // per_block)

    spread = as_bf16(
        holder_of(iota((EXPERTS, width), 1)) // 2 == iota((EXPERTS, width), 0)
    )

    def over_lines(table):
        return lax.dot_general(
            table, spread, (((0,), (0,)), ((), ())), preferred_element_type=jnp.float32
        )

    slots = over_lines(slot.astype(jnp.bfloat16))
    highs, lows = over_lines(high), over_lines(low)
    line = iota((TOK, width), 1)
    q, r = line // per_block, line % 8
    first = HELD * (holder_of(line) % 2)
    slots = slots - first.astype(jnp.float32)

    def hits(wanted):
        return (slots == wanted.astype(jnp.float32)) & (wanted >= 0)

    main = jnp.where(r < HELD, r, -1)
    rests = [jnp.where(r < HELD, -1, 2 * i + r - HELD) for i in range(3)]
    for j, wanted in enumerate([main] + rests):
        hit = hits(wanted)
        for i, part in enumerate((highs, lows)):
            out_ref[j, i * TOK : (i + 1) * TOK, :] = jnp.where(hit, part, 0.0).astype(jnp.bfloat16)
    odd = hits(jnp.where(q == 1, r - 2, -1))
    shared = hits(
        jnp.where((q == 1) & (r < 2), r, jnp.where((q == 2) & (r >= 6), r - 2, -1))
    )
    wanted = ((odd, 1, highs), (odd, 1, lows))
    wanted += ((shared, 1, highs), (shared, 1, lows), (shared, 2, highs), (shared, 2, lows))
    for i, (hit, b, part) in enumerate(wanted):
        odd_ref[i * TOK : (i + 1) * TOK, :] = jnp.where(hit, part, 0.0)[
            :, b * per_block : (b + 1) * per_block
        ].astype(jnp.bfloat16)


def combine_kernel(weights_ref, odd_ref, arrived_ref, residual_ref, out_ref, load_ref):
    quads = PEERS // QUAD
    per_block = 8 * quads

    def table(j, b=None, part=None):
        whole = weights_ref[j]
        if b is None:
            return whole
        return jnp.concatenate(
            [whole[:, : b * per_block], part, whole[:, (b + 1) * per_block :]], axis=1
        )


    def tile(t):
        return arrived_ref[:, t].reshape(8 * quads, LANES)

    def columns(c):
        return slice(c * LANES, (c + 1) * LANES)

    r = iota((8, 8 * quads), 1) % 8
    load = jnp.zeros((8, LANES), jnp.float32)
    for t, wanted in ((6, r == 0), (12, (r == 2) | (r == 4)), (18, r == 6)):
        load = load + jnp.dot(as_bf16(wanted), tile(t), preferred_element_type=jnp.float32)
    load_ref[...] = load[:1, :EXPERTS]
    sums = jnp.dot(odd_ref[2 * TOK :], tile(12), preferred_element_type=jnp.float32)
    none = jnp.zeros((2 * TOK, per_block), jnp.bfloat16)
    tails = [
        residual_ref[:, columns(6 + i)].astype(jnp.float32)
        + (sums[2 * i * TOK : (2 * i + 1) * TOK] + sums[(2 * i + 1) * TOK : (2 * i + 2) * TOK])
        for i in range(2)
    ]
    for c in range(6):
        lines = jnp.concatenate([tile(f + c) for f in FIRST], axis=0)
        main = table(0, 1, odd_ref[: 2 * TOK]) if c == 0 else table(0)
        rest = table(1 + c % 3, {0: 1, 5: 2}.get(c), none)
        sums = jnp.dot(
            jnp.concatenate([main, rest], axis=0), lines, preferred_element_type=jnp.float32
        )
        out_ref[:, columns(c)] = (
            residual_ref[:, columns(c)].astype(jnp.float32) + (sums[:TOK] + sums[TOK : 2 * TOK])
        ).astype(jnp.bfloat16)
        tails[c // 3] = tails[c // 3] + (sums[2 * TOK : 3 * TOK] + sums[3 * TOK :])
    for i in range(2):
        out_ref[:, columns(6 + i)] = tails[i].astype(jnp.bfloat16)


def per_device(residual, expert_ids, route_weights, expert_out):
    width = expert_out.shape[1]
    ids, routes = expert_ids.T, route_weights.T
    in_vmem = pl.BlockSpec(memory_space=pltpu.VMEM)
    in_hbm = pl.BlockSpec(memory_space=pltpu.HBM)
    steps = PEERS // (2 * OCT)
    packed = pl.pallas_call(
        pack_kernel,
        out_shape=jax.ShapeDtypeStruct((PEERS * LINES, LANES), jnp.bfloat16),
        in_specs=[in_hbm, in_hbm],
        out_specs=in_hbm,
        scratch_shapes=[
            pltpu.VMEM(expert_out.shape, jnp.bfloat16),
            pltpu.VMEM(ids.shape, jnp.int32),
            pltpu.VMEM((PEERS * LINES, LANES), jnp.bfloat16),
            pltpu.SemaphoreType.DMA((steps,)),
            pltpu.SemaphoreType.DMA,
            pltpu.SemaphoreType.DMA((steps,)),
        ],
        compiler_params=pltpu.CompilerParams(vmem_limit_bytes=60 * 2**20),
        name="pack",
    )(expert_out, ids)
    arrived = lax.all_to_all(
        packed.reshape(PEERS, LINES // 2, 2, LANES),
        "expert",
        split_axis=0,
        concat_axis=0,
        axis_index_groups=[list(range(PEERS - 1, -1, -1))],
        tiled=True,
    ).reshape(PEERS // QUAD, TILES, 8, LANES)
    weights, odd = pl.pallas_call(
        weights_kernel,
        out_shape=(
            jax.ShapeDtypeStruct((4, 2 * TOK, 8 * PEERS), jnp.bfloat16),
            jax.ShapeDtypeStruct((6 * TOK, 8 * PEERS // QUAD), jnp.bfloat16),
        ),
        in_specs=[in_vmem, in_vmem],
        out_specs=(in_vmem, in_vmem),
        compiler_params=pltpu.CompilerParams(vmem_limit_bytes=24 * 2**20),
        name="weights",
    )(ids, routes)
    mixed, load = pl.pallas_call(
        combine_kernel,
        out_shape=(
            jax.ShapeDtypeStruct((TOK, width), jnp.bfloat16),
            jax.ShapeDtypeStruct((1, EXPERTS), jnp.float32),
        ),
        in_specs=[in_vmem, in_vmem, in_vmem, in_vmem],
        out_specs=(in_vmem, in_vmem),
        compiler_params=pltpu.CompilerParams(vmem_limit_bytes=24 * 2**20),
        name="combine",
    )(weights, odd, arrived, residual)
    return mixed, load.reshape(EXPERTS)


def solution(mesh):
    placed = P(("dp", "expert"), None)
    return jax.shard_map(
        per_device,
        mesh=mesh,
        in_specs=(placed, placed, placed, placed),
        out_specs=(placed, P("dp")),
        check_vma=False,
    )
```

```python
import jax
import jax.numpy as jnp
from jax import lax
from jax.experimental import pallas as pl
from jax.experimental.pallas import tpu as pltpu
from jax.sharding import PartitionSpec as P

EXPERTS = 64
TOP = 8
TOK = 64
HELD = 6
PEERS = 128
LANES = 128
LINES = 50
QUAD = 4
TILES = QUAD * LINES // 8
OCT = 8
STACK = 32

FIRST = (0, 6, 13, 19)


def iota(shape, dim):
    return lax.broadcasted_iota(jnp.int32, shape, dim)


def as_bf16(mask):
    return mask.astype(jnp.float32).astype(jnp.bfloat16)


def pack_kernel(x_hbm, ids_hbm, out_hbm, x_ref, ids_ref, out_ref, x_sems, ids_sem, out_sems):
    rows = 2 * OCT * HELD
    steps = PEERS // (2 * OCT)
    x_copies, out_copies = [], []
    for g in range(steps):
        here = pl.ds(g * rows, rows)
        there = pl.ds((steps - 1 - g) * 2 * OCT * LINES, 2 * OCT * LINES)
        x_copies.append(pltpu.make_async_copy(x_hbm.at[here], x_ref.at[here], x_sems.at[g]))
        out_copies.append(
            pltpu.make_async_copy(out_ref.at[there], out_hbm.at[there], out_sems.at[g])
        )
    ids_copy = pltpu.make_async_copy(ids_hbm, ids_ref, ids_sem)
    ids_copy.start()
    for copy in x_copies:
        copy.start()
    block = (PEERS - 1 - lax.axis_index("expert")) % QUAD
    line = iota((QUAD * LINES, LANES), 0)
    owner = line * 0
    for b in range(1, QUAD):
        owner = jnp.where(line >= b * LINES, b, owner)
    place = line - owner * LINES + block * LINES
    t, r = place >> 3, place & 7
    c = t - jnp.where(t < 6, 0, jnp.where(t < 12, 6, jnp.where(t < 19, 13, 19)))
    main = jnp.where(t == 6, r - 2, r)
    rest = jnp.where(t == 12, jnp.where(r < 2, 0, 5), c)
    rest_row = 2 * jnp.where(rest >= 3, rest - 3, rest) + jnp.where(r < 2, r, r - 6)
    source = jnp.where((t != 12) & (main >= 0) & (main < HELD), STACK * c + main, 0)
    is_rest = ((t == 12) & ((r < 2) | (r >= 6))) | ((t != 6) & (t != 12) & (t != 18) & (r >= 6))
    source = jnp.where(is_rest, STACK * jnp.where(rest >= 3, 7, 6) + rest_row, source)
    source = source + HELD * (QUAD - 1 - owner)
    tally = ((t == 6) & (r < 2)) | ((t == 12) & (r >= 2) & (r < 6)) | ((t == 18) & (r >= 6))
    blank = (r & 1) == 1
    column = iota((QUAD * LINES, LANES), 1)
    picks = []
    for spare, shift in ((STACK - 8, 0), (0, 8)):
        here = jnp.where(tally, jnp.where(blank, -1, spare), source + shift)
        picks.append(
            jnp.concatenate([as_bf16(here == column), as_bf16(here == column + LANES)], axis=1)
        )
    ids_copy.wait()
    expert = iota((LANES, TOK), 0)
    named = jnp.zeros((LANES, TOK), jnp.float32)
    for k in range(TOP):
        named = named + (ids_ref[k : k + 1, :] == expert).astype(jnp.float32)
    counts = lax.dot_general(
        jnp.ones((16, TOK), jnp.bfloat16),
        named.astype(jnp.bfloat16),
        (((1,), (1,)), ((), ())),
        preferred_element_type=jnp.float32,
    )
    counts = jnp.concatenate([counts, counts], axis=1)
    upper = iota((16, 2 * LANES), 0) < 8
    for copy in x_copies:
        copy.wait()
    for g in range(steps):
        one = x_ref[pl.ds(g * rows, rows // 2), :]
        two = x_ref[pl.ds(g * rows + rows // 2, rows // 2), :]
        thirds = []
        for i in range(8):
            here = slice(i * LANES, (i + 1) * LANES)
            both = jnp.concatenate([one[:, here], two[:, here]], axis=1)
            thirds.append((both[:16], both[16:32], both[32:]))
        middle = thirds[0][1].astype(jnp.float32)
        spare = (
            jnp.where(upper, middle, counts).astype(jnp.bfloat16),
            jnp.where(upper, counts, middle).astype(jnp.bfloat16),
        )
        packed = []
        for half in range(2):
            stack = [thirds[0][0], spare[0]] if half == 0 else [spare[1], thirds[0][2]]
            for i in range(1, 8):
                stack += thirds[i][half : half + 2]
            packed.append(
                jnp.dot(
                    picks[half], jnp.concatenate(stack, axis=0), preferred_element_type=jnp.float32
                )
            )
        packed = jnp.concatenate(packed[::-1], axis=0).astype(jnp.bfloat16)
        start = (steps - 1 - g) * 2 * OCT * LINES
        out_ref[pl.ds(start + OCT * LINES, OCT * LINES), :] = packed[:, :LANES]
        out_ref[pl.ds(start, OCT * LINES), :] = packed[:, LANES:]
        if g % 2:
            out_copies[g - 1].start()
            out_copies[g].start()
    for copy in out_copies:
        copy.wait()


def weights_kernel(ids_ref, route_ref, out_ref, odd_ref):
    expert = iota((EXPERTS, TOK), 0)
    named = jnp.zeros((EXPERTS, TOK), jnp.float32)
    weight = jnp.zeros((EXPERTS, TOK), jnp.float32)
    for k in range(TOP):
        hit = ids_ref[k : k + 1, :] == expert
        named = jnp.where(hit, 1.0, named)
        weight = jnp.where(hit, route_ref[k : k + 1, :], weight)
    before = as_bf16(iota((TOK, TOK), 0) < iota((TOK, TOK), 1))
    slot = jnp.dot(named.astype(jnp.bfloat16), before, preferred_element_type=jnp.float32)
    slot = jnp.where(named > 0, slot, -1.0)
    high = weight.astype(jnp.bfloat16)
    low = (weight - high.astype(jnp.float32)).astype(jnp.bfloat16)
    width = 8 * PEERS
    per_block = width // QUAD

    def holder_of(line):
        return PEERS - 1 - (QUAD * ((line % per_block) // 8) + line // per_block)

    spread = as_bf16(
        holder_of(iota((EXPERTS, width), 1)) // 2 == iota((EXPERTS, width), 0)
    )

    def over_lines(table):
        return lax.dot_general(
            table, spread, (((0,), (0,)), ((), ())), preferred_element_type=jnp.float32
        )

    slots = over_lines(slot.astype(jnp.bfloat16))
    highs, lows = over_lines(high), over_lines(low)
    line = iota((TOK, width), 1)
    q, r = line // per_block, line % 8
    first = HELD * (holder_of(line) % 2)
    slots = slots - first.astype(jnp.float32)

    def hits(wanted):
        return (slots == wanted.astype(jnp.float32)) & (wanted >= 0)

    main = jnp.where(r < HELD, r, -1)
    rests = [jnp.where(r < HELD, -1, 2 * i + r - HELD) for i in range(3)]
    for j, wanted in enumerate([main] + rests):
        hit = hits(wanted)
        for i, part in enumerate((highs, lows)):
            out_ref[j, i * TOK : (i + 1) * TOK, :] = jnp.where(hit, part, 0.0).astype(jnp.bfloat16)
    odd = hits(jnp.where(q == 1, r - 2, -1))
    shared = hits(
        jnp.where((q == 1) & (r < 2), r, jnp.where((q == 2) & (r >= 6), r - 2, -1))
    )
    wanted = ((odd, 1, highs), (odd, 1, lows))
    wanted += ((shared, 1, highs), (shared, 1, lows), (shared, 2, highs), (shared, 2, lows))
    for i, (hit, b, part) in enumerate(wanted):
        odd_ref[i * TOK : (i + 1) * TOK, :] = jnp.where(hit, part, 0.0)[
            :, b * per_block : (b + 1) * per_block
        ].astype(jnp.bfloat16)


def combine_kernel(weights_ref, odd_ref, arrived_ref, residual_ref, out_ref, load_ref):
    quads = PEERS // QUAD
    per_block = 8 * quads

    def tile(t):
        return arrived_ref[:, t].reshape(8 * quads, LANES)

    def columns(c):
        return slice(c * LANES, (c + 1) * LANES)

    r = iota((8, 8 * quads), 1) % 8
    load = jnp.zeros((8, LANES), jnp.float32)
    for t, wanted in ((6, r == 0), (12, (r == 2) | (r == 4)), (18, r == 6)):
        load = load + jnp.dot(as_bf16(wanted), tile(t), preferred_element_type=jnp.float32)
    load_ref[...] = load[:1, :EXPERTS]
    sums = jnp.dot(odd_ref[2 * TOK :], tile(12), preferred_element_type=jnp.float32)
    tails = [
        residual_ref[:, columns(6 + i)].astype(jnp.float32)
        + (sums[2 * i * TOK : (2 * i + 1) * TOK] + sums[(2 * i + 1) * TOK : (2 * i + 2) * TOK])
        for i in range(2)
    ]
    none = jnp.zeros((per_block, LANES), jnp.bfloat16)
    odd = {
        0: jnp.dot(odd_ref[: 2 * TOK], tile(6), preferred_element_type=jnp.float32),
        5: jnp.dot(
            weights_ref[0, :, 2 * per_block : 3 * per_block],
            tile(18),
            preferred_element_type=jnp.float32,
        ),
    }
    for c in range(3):
        lines = jnp.concatenate(
            [
                jnp.concatenate(
                    [none if f + i in (6, 18) else tile(f + i) for i in (c, c + 3)], axis=1
                )
                for f in FIRST
            ],
            axis=0,
        )
        sums = jnp.dot(
            jnp.concatenate([weights_ref[0], weights_ref[1 + c]], axis=0),
            lines,
            preferred_element_type=jnp.float32,
        )
        for i in range(2):
            part = sums[:, columns(i)]
            main = part[:TOK] + part[TOK : 2 * TOK]
            if c + 3 * i in odd:
                main = main + (odd[c + 3 * i][:TOK] + odd[c + 3 * i][TOK:])
            here = columns(c + 3 * i)
            out_ref[:, here] = (residual_ref[:, here].astype(jnp.float32) + main).astype(
                jnp.bfloat16
            )
            tails[i] = tails[i] + (part[2 * TOK : 3 * TOK] + part[3 * TOK :])
    for i in range(2):
        out_ref[:, columns(6 + i)] = tails[i].astype(jnp.bfloat16)


def per_device(residual, expert_ids, route_weights, expert_out):
    width = expert_out.shape[1]
    ids, routes = expert_ids.T, route_weights.T
    in_vmem = pl.BlockSpec(memory_space=pltpu.VMEM)
    in_hbm = pl.BlockSpec(memory_space=pltpu.HBM)
    steps = PEERS // (2 * OCT)
    packed = pl.pallas_call(
        pack_kernel,
        out_shape=jax.ShapeDtypeStruct((PEERS * LINES, LANES), jnp.bfloat16),
        in_specs=[in_hbm, in_hbm],
        out_specs=in_hbm,
        scratch_shapes=[
            pltpu.VMEM(expert_out.shape, jnp.bfloat16),
            pltpu.VMEM(ids.shape, jnp.int32),
            pltpu.VMEM((PEERS * LINES, LANES), jnp.bfloat16),
            pltpu.SemaphoreType.DMA((steps,)),
            pltpu.SemaphoreType.DMA,
            pltpu.SemaphoreType.DMA((steps,)),
        ],
        compiler_params=pltpu.CompilerParams(vmem_limit_bytes=60 * 2**20),
        name="pack",
    )(expert_out, ids)
    arrived = lax.all_to_all(
        packed.reshape(PEERS, LINES // 2, 2, LANES),
        "expert",
        split_axis=0,
        concat_axis=0,
        axis_index_groups=[list(range(PEERS - 1, -1, -1))],
        tiled=True,
    ).reshape(PEERS // QUAD, TILES, 8, LANES)
    weights, odd = pl.pallas_call(
        weights_kernel,
        out_shape=(
            jax.ShapeDtypeStruct((4, 2 * TOK, 8 * PEERS), jnp.bfloat16),
            jax.ShapeDtypeStruct((6 * TOK, 8 * PEERS // QUAD), jnp.bfloat16),
        ),
        in_specs=[in_vmem, in_vmem],
        out_specs=(in_vmem, in_vmem),
        compiler_params=pltpu.CompilerParams(vmem_limit_bytes=24 * 2**20),
        name="weights",
    )(ids, routes)
    mixed, load = pl.pallas_call(
        combine_kernel,
        out_shape=(
            jax.ShapeDtypeStruct((TOK, width), jnp.bfloat16),
            jax.ShapeDtypeStruct((1, EXPERTS), jnp.float32),
        ),
        in_specs=[in_vmem, in_vmem, in_vmem, in_vmem],
        out_specs=(in_vmem, in_vmem),
        compiler_params=pltpu.CompilerParams(vmem_limit_bytes=24 * 2**20),
        name="combine",
    )(weights, odd, arrived, residual)
    return mixed, load.reshape(EXPERTS)


def solution(mesh):
    placed = P(("dp", "expert"), None)
    return jax.shard_map(
        per_device,
        mesh=mesh,
        in_specs=(placed, placed, placed, placed),
        out_specs=(placed, P("dp")),
        check_vma=False,
    )
```

```python
import jax
import jax.numpy as jnp
from jax import lax
from jax.experimental import pallas as pl
from jax.experimental.pallas import tpu as pltpu
from jax.sharding import PartitionSpec as P

EXPERTS = 64
TOP = 8
TOK = 64
HELD = 6
PEERS = 128
LANES = 128
LINES = 50
QUAD = 4
TILES = QUAD * LINES // 8
OCT = 8
STACK = 32

FIRST = (0, 6, 13, 19)


def iota(shape, dim):
    return lax.broadcasted_iota(jnp.int32, shape, dim)


def as_bf16(mask):
    return mask.astype(jnp.float32).astype(jnp.bfloat16)


def pack_kernel(x_hbm, ids_hbm, out_hbm, x_ref, ids_ref, out_ref, x_sems, ids_sem, out_sems):
    rows = 2 * OCT * HELD
    steps = PEERS // (2 * OCT)
    x_copies, out_copies = [], []
    for g in range(steps):
        here = pl.ds(g * rows, rows)
        there = pl.ds((steps - 1 - g) * 2 * OCT * LINES, 2 * OCT * LINES)
        x_copies.append(pltpu.make_async_copy(x_hbm.at[here], x_ref.at[here], x_sems.at[g]))
        out_copies.append(
            pltpu.make_async_copy(out_ref.at[there], out_hbm.at[there], out_sems.at[g])
        )
    ids_copy = pltpu.make_async_copy(ids_hbm, ids_ref, ids_sem)
    ids_copy.start()
    for g, copy in enumerate(x_copies):
        copy.start(priority=2 * g // steps)
    block = (PEERS - 1 - lax.axis_index("expert")) % QUAD
    line = iota((QUAD * LINES, LANES), 0)
    owner = line * 0
    for b in range(1, QUAD):
        owner = jnp.where(line >= b * LINES, b, owner)
    place = line - owner * LINES + block * LINES
    t, r = place >> 3, place & 7
    c = t - jnp.where(t < 6, 0, jnp.where(t < 12, 6, jnp.where(t < 19, 13, 19)))
    main = jnp.where(t == 6, r - 2, r)
    rest = jnp.where(t == 12, jnp.where(r < 2, 0, 5), c)
    rest_row = 2 * jnp.where(rest >= 3, rest - 3, rest) + jnp.where(r < 2, r, r - 6)
    source = jnp.where((t != 12) & (main >= 0) & (main < HELD), STACK * c + main, 0)
    is_rest = ((t == 12) & ((r < 2) | (r >= 6))) | ((t != 6) & (t != 12) & (t != 18) & (r >= 6))
    source = jnp.where(is_rest, STACK * jnp.where(rest >= 3, 7, 6) + rest_row, source)
    source = source + HELD * (QUAD - 1 - owner)
    tally = ((t == 6) & (r < 2)) | ((t == 12) & (r >= 2) & (r < 6)) | ((t == 18) & (r >= 6))
    blank = (r & 1) == 1
    column = iota((QUAD * LINES, LANES), 1)
    picks = []
    for spare, shift in ((STACK - 8, 0), (0, 8)):
        here = jnp.where(tally, jnp.where(blank, -1, spare), source + shift)
        picks.append(
            jnp.concatenate([as_bf16(here == column), as_bf16(here == column + LANES)], axis=1)
        )
    ids_copy.wait()
    expert = iota((LANES, TOK), 0)
    named = jnp.zeros((LANES, TOK), jnp.float32)
    for k in range(TOP):
        named = named + (ids_ref[k : k + 1, :] == expert).astype(jnp.float32)
    counts = lax.dot_general(
        jnp.ones((16, TOK), jnp.bfloat16),
        named.astype(jnp.bfloat16),
        (((1,), (1,)), ((), ())),
        preferred_element_type=jnp.float32,
    )
    counts = jnp.concatenate([counts, counts], axis=1)
    upper = iota((16, 2 * LANES), 0) < 8
    for g in range(steps):
        if g % (steps // 2) == 0:
            for copy in x_copies[g : g + steps // 2]:
                copy.wait()
        one = x_ref[pl.ds(g * rows, rows // 2), :]
        two = x_ref[pl.ds(g * rows + rows // 2, rows // 2), :]
        thirds = []
        for i in range(8):
            here = slice(i * LANES, (i + 1) * LANES)
            both = jnp.concatenate([one[:, here], two[:, here]], axis=1)
            thirds.append((both[:16], both[16:32], both[32:]))
        middle = thirds[0][1].astype(jnp.float32)
        spare = (
            jnp.where(upper, middle, counts).astype(jnp.bfloat16),
            jnp.where(upper, counts, middle).astype(jnp.bfloat16),
        )
        packed = []
        for half in range(2):
            stack = [thirds[0][0], spare[0]] if half == 0 else [spare[1], thirds[0][2]]
            for i in range(1, 8):
                stack += thirds[i][half : half + 2]
            packed.append(
                jnp.dot(
                    picks[half], jnp.concatenate(stack, axis=0), preferred_element_type=jnp.float32
                )
            )
        packed = jnp.concatenate(packed[::-1], axis=0).astype(jnp.bfloat16)
        start = (steps - 1 - g) * 2 * OCT * LINES
        out_ref[pl.ds(start + OCT * LINES, OCT * LINES), :] = packed[:, :LANES]
        out_ref[pl.ds(start, OCT * LINES), :] = packed[:, LANES:]
        out_copies[g].start()
    for copy in out_copies:
        copy.wait()


def weights_kernel(ids_ref, route_ref, out_ref, odd_ref):
    expert = iota((EXPERTS, TOK), 0)
    named = jnp.zeros((EXPERTS, TOK), jnp.float32)
    weight = jnp.zeros((EXPERTS, TOK), jnp.float32)
    for k in range(TOP):
        hit = ids_ref[k : k + 1, :] == expert
        named = jnp.where(hit, 1.0, named)
        weight = jnp.where(hit, route_ref[k : k + 1, :], weight)
    before = as_bf16(iota((TOK, TOK), 0) < iota((TOK, TOK), 1))
    slot = jnp.dot(named.astype(jnp.bfloat16), before, preferred_element_type=jnp.float32)
    slot = jnp.where(named > 0, slot, -1.0)
    high = weight.astype(jnp.bfloat16)
    low = (weight - high.astype(jnp.float32)).astype(jnp.bfloat16)
    width = 8 * PEERS
    per_block = width // QUAD

    def holder_of(line):
        return PEERS - 1 - (QUAD * ((line % per_block) // 8) + line // per_block)

    spread = as_bf16(
        holder_of(iota((EXPERTS, width), 1)) // 2 == iota((EXPERTS, width), 0)
    )

    def over_lines(table):
        return lax.dot_general(
            table, spread, (((0,), (0,)), ((), ())), preferred_element_type=jnp.float32
        )

    slots = over_lines(slot.astype(jnp.bfloat16))
    highs, lows = over_lines(high), over_lines(low)
    line = iota((TOK, width), 1)
    q, r = line // per_block, line % 8
    first = HELD * (holder_of(line) % 2)
    slots = slots - first.astype(jnp.float32)

    def hits(wanted):
        return (slots == wanted.astype(jnp.float32)) & (wanted >= 0)

    main = jnp.where(r < HELD, r, -1)
    rests = [jnp.where(r < HELD, -1, 2 * i + r - HELD) for i in range(3)]
    for j, wanted in enumerate([main] + rests):
        hit = hits(wanted)
        for i, part in enumerate((highs, lows)):
            out_ref[j, i * TOK : (i + 1) * TOK, :] = jnp.where(hit, part, 0.0).astype(jnp.bfloat16)
    odd = hits(jnp.where(q == 1, r - 2, -1))
    shared = hits(
        jnp.where((q == 1) & (r < 2), r, jnp.where((q == 2) & (r >= 6), r - 2, -1))
    )
    wanted = ((odd, 1, highs), (odd, 1, lows))
    wanted += ((shared, 1, highs), (shared, 1, lows), (shared, 2, highs), (shared, 2, lows))
    for i, (hit, b, part) in enumerate(wanted):
        odd_ref[i * TOK : (i + 1) * TOK, :] = jnp.where(hit, part, 0.0)[
            :, b * per_block : (b + 1) * per_block
        ].astype(jnp.bfloat16)


def combine_kernel(weights_ref, odd_ref, arrived_ref, residual_ref, out_ref, load_ref):
    quads = PEERS // QUAD
    per_block = 8 * quads

    def tile(t):
        return arrived_ref[:, t].reshape(8 * quads, LANES)

    def columns(c):
        return slice(c * LANES, (c + 1) * LANES)

    r = iota((8, 8 * quads), 1) % 8
    load = jnp.zeros((8, LANES), jnp.float32)
    for t, wanted in ((6, r == 0), (12, (r == 2) | (r == 4)), (18, r == 6)):
        load = load + jnp.dot(as_bf16(wanted), tile(t), preferred_element_type=jnp.float32)
    load_ref[...] = load[:1, :EXPERTS]
    sums = jnp.dot(odd_ref[2 * TOK :], tile(12), preferred_element_type=jnp.float32)
    tails = [
        residual_ref[:, columns(6 + i)].astype(jnp.float32)
        + (sums[2 * i * TOK : (2 * i + 1) * TOK] + sums[(2 * i + 1) * TOK : (2 * i + 2) * TOK])
        for i in range(2)
    ]
    none = jnp.zeros((per_block, LANES), jnp.bfloat16)
    odd = {
        0: jnp.dot(odd_ref[: 2 * TOK], tile(6), preferred_element_type=jnp.float32),
        5: jnp.dot(
            weights_ref[0, :, 2 * per_block : 3 * per_block],
            tile(18),
            preferred_element_type=jnp.float32,
        ),
    }
    for c in range(3):
        lines = jnp.concatenate(
            [
                jnp.concatenate(
                    [none if f + i in (6, 18) else tile(f + i) for i in (c, c + 3)], axis=1
                )
                for f in FIRST
            ],
            axis=0,
        )
        sums = jnp.dot(
            jnp.concatenate([weights_ref[0], weights_ref[1 + c]], axis=0),
            lines,
            preferred_element_type=jnp.float32,
        )
        for i in range(2):
            part = sums[:, columns(i)]
            main = part[:TOK] + part[TOK : 2 * TOK]
            if c + 3 * i in odd:
                main = main + (odd[c + 3 * i][:TOK] + odd[c + 3 * i][TOK:])
            here = columns(c + 3 * i)
            out_ref[:, here] = (residual_ref[:, here].astype(jnp.float32) + main).astype(
                jnp.bfloat16
            )
            tails[i] = tails[i] + (part[2 * TOK : 3 * TOK] + part[3 * TOK :])
    for i in range(2):
        out_ref[:, columns(6 + i)] = tails[i].astype(jnp.bfloat16)


def per_device(residual, expert_ids, route_weights, expert_out):
    width = expert_out.shape[1]
    ids, routes = expert_ids.T, route_weights.T
    in_vmem = pl.BlockSpec(memory_space=pltpu.VMEM)
    in_hbm = pl.BlockSpec(memory_space=pltpu.HBM)
    steps = PEERS // (2 * OCT)
    packed = pl.pallas_call(
        pack_kernel,
        out_shape=jax.ShapeDtypeStruct((PEERS * LINES, LANES), jnp.bfloat16),
        in_specs=[in_hbm, in_hbm],
        out_specs=in_hbm,
        scratch_shapes=[
            pltpu.VMEM(expert_out.shape, jnp.bfloat16),
            pltpu.VMEM(ids.shape, jnp.int32),
            pltpu.VMEM((PEERS * LINES, LANES), jnp.bfloat16),
            pltpu.SemaphoreType.DMA((steps,)),
            pltpu.SemaphoreType.DMA,
            pltpu.SemaphoreType.DMA((steps,)),
        ],
        compiler_params=pltpu.CompilerParams(vmem_limit_bytes=60 * 2**20),
        name="pack",
    )(expert_out, ids)
    arrived = lax.all_to_all(
        packed.reshape(PEERS, LINES // 2, 2, LANES),
        "expert",
        split_axis=0,
        concat_axis=0,
        axis_index_groups=[list(range(PEERS - 1, -1, -1))],
        tiled=True,
    ).reshape(PEERS // QUAD, TILES, 8, LANES)
    weights, odd = pl.pallas_call(
        weights_kernel,
        out_shape=(
            jax.ShapeDtypeStruct((4, 2 * TOK, 8 * PEERS), jnp.bfloat16),
            jax.ShapeDtypeStruct((6 * TOK, 8 * PEERS // QUAD), jnp.bfloat16),
        ),
        in_specs=[in_vmem, in_vmem],
        out_specs=(in_vmem, in_vmem),
        compiler_params=pltpu.CompilerParams(vmem_limit_bytes=24 * 2**20),
        name="weights",
    )(ids, routes)
    mixed, load = pl.pallas_call(
        combine_kernel,
        out_shape=(
            jax.ShapeDtypeStruct((TOK, width), jnp.bfloat16),
            jax.ShapeDtypeStruct((1, EXPERTS), jnp.float32),
        ),
        in_specs=[in_vmem, in_vmem, in_vmem, in_vmem],
        out_specs=(in_vmem, in_vmem),
        compiler_params=pltpu.CompilerParams(vmem_limit_bytes=24 * 2**20),
        name="combine",
    )(weights, odd, arrived, residual)
    return mixed, load.reshape(EXPERTS)


def solution(mesh):
    placed = P(("dp", "expert"), None)
    return jax.shard_map(
        per_device,
        mesh=mesh,
        in_specs=(placed, placed, placed, placed),
        out_specs=(placed, P("dp")),
        check_vma=False,
    )
```

```python
import jax
import jax.numpy as jnp
from jax import lax
from jax.experimental import pallas as pl
from jax.experimental.pallas import tpu as pltpu
from jax.sharding import PartitionSpec as P

EXPERTS = 64
TOP = 8
TOK = 64
HELD = 6
PEERS = 128
LANES = 128
LINES = 50
QUAD = 4
TILES = QUAD * LINES // 8
OCT = 8
STACK = 32

FIRST = (0, 6, 13, 19)


def iota(shape, dim):
    return lax.broadcasted_iota(jnp.int32, shape, dim)


def as_bf16(mask):
    return mask.astype(jnp.float32).astype(jnp.bfloat16)


def pack_kernel(x_hbm, ids_hbm, out_hbm, x_ref, ids_ref, out_ref, x_sems, ids_sem, out_sems):
    rows = 2 * OCT * HELD
    steps = PEERS // (2 * OCT)
    x_copies, out_copies = {}, []
    for i, (g, end) in enumerate(((0, 3), (3, steps))):
        here = pl.ds(g * rows, (end - g) * rows)
        x_copies[g] = pltpu.make_async_copy(x_hbm.at[here], x_ref.at[here], x_sems.at[i])
    for g in range(steps):
        there = pl.ds((steps - 1 - g) * 2 * OCT * LINES, 2 * OCT * LINES)
        out_copies.append(
            pltpu.make_async_copy(out_ref.at[there], out_hbm.at[there], out_sems.at[g])
        )
    ids_copy = pltpu.make_async_copy(ids_hbm, ids_ref, ids_sem)
    ids_copy.start()
    for i, copy in enumerate(x_copies.values()):
        copy.start(priority=i)
    block = (PEERS - 1 - lax.axis_index("expert")) % QUAD
    line = iota((QUAD * LINES, LANES), 0)
    owner = line * 0
    for b in range(1, QUAD):
        owner = jnp.where(line >= b * LINES, b, owner)
    place = line - owner * LINES + block * LINES
    t, r = place >> 3, place & 7
    c = t - jnp.where(t < 6, 0, jnp.where(t < 12, 6, jnp.where(t < 19, 13, 19)))
    main = jnp.where(t == 6, r - 2, r)
    rest = jnp.where(t == 12, jnp.where(r < 2, 0, 5), c)
    rest_row = 2 * jnp.where(rest >= 3, rest - 3, rest) + jnp.where(r < 2, r, r - 6)
    source = jnp.where((t != 12) & (main >= 0) & (main < HELD), STACK * c + main, 0)
    is_rest = ((t == 12) & ((r < 2) | (r >= 6))) | ((t != 6) & (t != 12) & (t != 18) & (r >= 6))
    source = jnp.where(is_rest, STACK * jnp.where(rest >= 3, 7, 6) + rest_row, source)
    source = source + HELD * (QUAD - 1 - owner)
    tally = ((t == 6) & (r < 2)) | ((t == 12) & (r >= 2) & (r < 6)) | ((t == 18) & (r >= 6))
    blank = (r & 1) == 1
    column = iota((QUAD * LINES, LANES), 1)
    picks = []
    for spare, shift in ((STACK - 8, 0), (0, 8)):
        here = jnp.where(tally, jnp.where(blank, -1, spare), source + shift)
        picks.append(
            jnp.concatenate([as_bf16(here == column), as_bf16(here == column + LANES)], axis=1)
        )
    ids_copy.wait()
    expert = iota((LANES, TOK), 0)
    named = jnp.zeros((LANES, TOK), jnp.float32)
    for k in range(TOP):
        named = named + (ids_ref[k : k + 1, :] == expert).astype(jnp.float32)
    counts = lax.dot_general(
        jnp.ones((16, TOK), jnp.bfloat16),
        named.astype(jnp.bfloat16),
        (((1,), (1,)), ((), ())),
        preferred_element_type=jnp.float32,
    )
    counts = jnp.concatenate([counts, counts], axis=1)
    upper = iota((16, 2 * LANES), 0) < 8
    for g in range(steps):
        if g in x_copies:
            x_copies[g].wait()
        one = x_ref[pl.ds(g * rows, rows // 2), :]
        two = x_ref[pl.ds(g * rows + rows // 2, rows // 2), :]
        thirds = []
        for i in range(8):
            here = slice(i * LANES, (i + 1) * LANES)
            both = jnp.concatenate([one[:, here], two[:, here]], axis=1)
            thirds.append((both[:16], both[16:32], both[32:]))
        middle = thirds[0][1].astype(jnp.float32)
        spare = (
            jnp.where(upper, middle, counts).astype(jnp.bfloat16),
            jnp.where(upper, counts, middle).astype(jnp.bfloat16),
        )
        packed = []
        for half in range(2):
            stack = [thirds[0][0], spare[0]] if half == 0 else [spare[1], thirds[0][2]]
            for i in range(1, 8):
                stack += thirds[i][half : half + 2]
            packed.append(
                jnp.dot(
                    picks[half], jnp.concatenate(stack, axis=0), preferred_element_type=jnp.float32
                )
            )
        packed = jnp.concatenate(packed[::-1], axis=0).astype(jnp.bfloat16)
        start = (steps - 1 - g) * 2 * OCT * LINES
        out_ref[pl.ds(start + OCT * LINES, OCT * LINES), :] = packed[:, :LANES]
        out_ref[pl.ds(start, OCT * LINES), :] = packed[:, LANES:]
        out_copies[g].start()
    for copy in out_copies:
        copy.wait()


def weights_kernel(ids_ref, route_ref, out_ref, odd_ref):
    expert = iota((EXPERTS, TOK), 0)
    named = jnp.zeros((EXPERTS, TOK), jnp.float32)
    weight = jnp.zeros((EXPERTS, TOK), jnp.float32)
    for k in range(TOP):
        hit = ids_ref[k : k + 1, :] == expert
        named = jnp.where(hit, 1.0, named)
        weight = jnp.where(hit, route_ref[k : k + 1, :], weight)
    before = as_bf16(iota((TOK, TOK), 0) < iota((TOK, TOK), 1))
    slot = jnp.dot(named.astype(jnp.bfloat16), before, preferred_element_type=jnp.float32)
    slot = jnp.where(named > 0, slot, -1.0)
    high = weight.astype(jnp.bfloat16)
    low = (weight - high.astype(jnp.float32)).astype(jnp.bfloat16)
    width = 8 * PEERS
    per_block = width // QUAD

    def holder_of(line):
        return PEERS - 1 - (QUAD * ((line % per_block) // 8) + line // per_block)

    spread = as_bf16(
        holder_of(iota((EXPERTS, width), 1)) // 2 == iota((EXPERTS, width), 0)
    )

    def over_lines(table):
        return lax.dot_general(
            table, spread, (((0,), (0,)), ((), ())), preferred_element_type=jnp.float32
        )

    slots = over_lines(slot.astype(jnp.bfloat16))
    highs, lows = over_lines(high), over_lines(low)
    line = iota((TOK, width), 1)
    q, r = line // per_block, line % 8
    first = HELD * (holder_of(line) % 2)
    slots = slots - first.astype(jnp.float32)

    def hits(wanted):
        return (slots == wanted.astype(jnp.float32)) & (wanted >= 0)

    main = jnp.where(r < HELD, r, -1)
    rests = [jnp.where(r < HELD, -1, 2 * i + r - HELD) for i in range(3)]
    for j, wanted in enumerate([main] + rests):
        hit = hits(wanted)
        for i, part in enumerate((highs, lows)):
            out_ref[j, i * TOK : (i + 1) * TOK, :] = jnp.where(hit, part, 0.0).astype(jnp.bfloat16)
    odd = hits(jnp.where(q == 1, r - 2, -1))
    shared = hits(
        jnp.where((q == 1) & (r < 2), r, jnp.where((q == 2) & (r >= 6), r - 2, -1))
    )
    wanted = ((odd, 1, highs), (odd, 1, lows))
    wanted += ((shared, 1, highs), (shared, 1, lows), (shared, 2, highs), (shared, 2, lows))
    for i, (hit, b, part) in enumerate(wanted):
        odd_ref[i * TOK : (i + 1) * TOK, :] = jnp.where(hit, part, 0.0)[
            :, b * per_block : (b + 1) * per_block
        ].astype(jnp.bfloat16)


def combine_kernel(weights_ref, odd_ref, arrived_ref, residual_ref, out_ref, load_ref):
    quads = PEERS // QUAD
    per_block = 8 * quads

    def tile(t):
        return arrived_ref[:, t].reshape(8 * quads, LANES)

    def columns(c):
        return slice(c * LANES, (c + 1) * LANES)

    r = iota((8, 8 * quads), 1) % 8
    load = jnp.zeros((8, LANES), jnp.float32)
    for t, wanted in ((6, r == 0), (12, (r == 2) | (r == 4)), (18, r == 6)):
        load = load + jnp.dot(as_bf16(wanted), tile(t), preferred_element_type=jnp.float32)
    load_ref[...] = load[:1, :EXPERTS]
    sums = jnp.dot(odd_ref[2 * TOK :], tile(12), preferred_element_type=jnp.float32)
    tails = [
        residual_ref[:, columns(6 + i)].astype(jnp.float32)
        + (sums[2 * i * TOK : (2 * i + 1) * TOK] + sums[(2 * i + 1) * TOK : (2 * i + 2) * TOK])
        for i in range(2)
    ]
    none = jnp.zeros((per_block, LANES), jnp.bfloat16)
    odd = {
        0: jnp.dot(odd_ref[: 2 * TOK], tile(6), preferred_element_type=jnp.float32),
        5: jnp.dot(
            weights_ref[0, :, 2 * per_block : 3 * per_block],
            tile(18),
            preferred_element_type=jnp.float32,
        ),
    }
    for c in range(3):
        lines = jnp.concatenate(
            [
                jnp.concatenate(
                    [none if f + i in (6, 18) else tile(f + i) for i in (c, c + 3)], axis=1
                )
                for f in FIRST
            ],
            axis=0,
        )
        sums = jnp.dot(
            jnp.concatenate([weights_ref[0], weights_ref[1 + c]], axis=0),
            lines,
            preferred_element_type=jnp.float32,
        )
        for i in range(2):
            part = sums[:, columns(i)]
            main = part[:TOK] + part[TOK : 2 * TOK]
            if c + 3 * i in odd:
                main = main + (odd[c + 3 * i][:TOK] + odd[c + 3 * i][TOK:])
            here = columns(c + 3 * i)
            out_ref[:, here] = (residual_ref[:, here].astype(jnp.float32) + main).astype(
                jnp.bfloat16
            )
            tails[i] = tails[i] + (part[2 * TOK : 3 * TOK] + part[3 * TOK :])
    for i in range(2):
        out_ref[:, columns(6 + i)] = tails[i].astype(jnp.bfloat16)


def per_device(residual, expert_ids, route_weights, expert_out):
    width = expert_out.shape[1]
    ids, routes = expert_ids.T, route_weights.T
    in_vmem = pl.BlockSpec(memory_space=pltpu.VMEM)
    in_hbm = pl.BlockSpec(memory_space=pltpu.HBM)
    steps = PEERS // (2 * OCT)
    packed = pl.pallas_call(
        pack_kernel,
        out_shape=jax.ShapeDtypeStruct((PEERS * LINES, LANES), jnp.bfloat16),
        in_specs=[in_hbm, in_hbm],
        out_specs=in_hbm,
        scratch_shapes=[
            pltpu.VMEM(expert_out.shape, jnp.bfloat16),
            pltpu.VMEM(ids.shape, jnp.int32),
            pltpu.VMEM((PEERS * LINES, LANES), jnp.bfloat16),
            pltpu.SemaphoreType.DMA((2,)),
            pltpu.SemaphoreType.DMA,
            pltpu.SemaphoreType.DMA((steps,)),
        ],
        compiler_params=pltpu.CompilerParams(vmem_limit_bytes=60 * 2**20),
        name="pack",
    )(expert_out, ids)
    arrived = lax.all_to_all(
        packed.reshape(PEERS, LINES // 2, 2, LANES),
        "expert",
        split_axis=0,
        concat_axis=0,
        axis_index_groups=[list(range(PEERS - 1, -1, -1))],
        tiled=True,
    ).reshape(PEERS // QUAD, TILES, 8, LANES)
    weights, odd = pl.pallas_call(
        weights_kernel,
        out_shape=(
            jax.ShapeDtypeStruct((4, 2 * TOK, 8 * PEERS), jnp.bfloat16),
            jax.ShapeDtypeStruct((6 * TOK, 8 * PEERS // QUAD), jnp.bfloat16),
        ),
        in_specs=[in_vmem, in_vmem],
        out_specs=(in_vmem, in_vmem),
        compiler_params=pltpu.CompilerParams(vmem_limit_bytes=24 * 2**20),
        name="weights",
    )(ids, routes)
    mixed, load = pl.pallas_call(
        combine_kernel,
        out_shape=(
            jax.ShapeDtypeStruct((TOK, width), jnp.bfloat16),
            jax.ShapeDtypeStruct((1, EXPERTS), jnp.float32),
        ),
        in_specs=[in_vmem, in_vmem, in_vmem, in_vmem],
        out_specs=(in_vmem, in_vmem),
        compiler_params=pltpu.CompilerParams(vmem_limit_bytes=24 * 2**20),
        name="combine",
    )(weights, odd, arrived, residual)
    return mixed, load.reshape(EXPERTS)


def solution(mesh):
    placed = P(("dp", "expert"), None)
    return jax.shard_map(
        per_device,
        mesh=mesh,
        in_specs=(placed, placed, placed, placed),
        out_specs=(placed, P("dp")),
        check_vma=False,
    )
```

```python
import jax
import jax.numpy as jnp
from jax import lax
from jax.experimental import pallas as pl
from jax.experimental.pallas import tpu as pltpu
from jax.sharding import PartitionSpec as P

EXPERTS = 64
TOP = 8
TOK = 64
HELD = 6
PEERS = 128
LANES = 128
LINES = 50
QUAD = 4
TILES = QUAD * LINES // 8
OCT = 8
STACK = 32

FIRST = (0, 6, 13, 19)


def iota(shape, dim):
    return lax.broadcasted_iota(jnp.int32, shape, dim)


def as_bf16(mask):
    return mask.astype(jnp.float32).astype(jnp.bfloat16)


def pack_kernel(x_hbm, ids_hbm, out_hbm, x_ref, ids_ref, out_ref, x_sems, ids_sem, out_sems):
    rows = 2 * OCT * HELD
    steps = PEERS // (2 * OCT)
    x_copies, out_copies = {}, []
    for i, (g, end) in enumerate(((0, 3), (3, steps))):
        here = pl.ds(g * rows, (end - g) * rows)
        x_copies[g] = pltpu.make_async_copy(x_hbm.at[here], x_ref.at[here], x_sems.at[i])
    for g in range(steps):
        there = pl.ds((steps - 1 - g) * 2 * OCT * LINES, 2 * OCT * LINES)
        out_copies.append(
            pltpu.make_async_copy(out_ref.at[there], out_hbm.at[there], out_sems.at[g])
        )
    ids_copy = pltpu.make_async_copy(ids_hbm, ids_ref, ids_sem)
    ids_copy.start()
    for i, copy in enumerate(x_copies.values()):
        copy.start(priority=i)
    block = (PEERS - 1 - lax.axis_index("expert")) % QUAD
    line = iota((QUAD * LINES, LANES), 0)
    owner = line * 0
    for b in range(1, QUAD):
        owner = jnp.where(line >= b * LINES, b, owner)
    place = line - owner * LINES + block * LINES
    t, r = place >> 3, place & 7
    c = t - jnp.where(t < 6, 0, jnp.where(t < 12, 6, jnp.where(t < 19, 13, 19)))
    main = jnp.where(t == 6, r - 2, r)
    rest = jnp.where(t == 12, jnp.where(r < 2, 0, 5), c)
    rest_row = 2 * jnp.where(rest >= 3, rest - 3, rest) + jnp.where(r < 2, r, r - 6)
    source = jnp.where((t != 12) & (main >= 0) & (main < HELD), STACK * c + main, 0)
    is_rest = ((t == 12) & ((r < 2) | (r >= 6))) | ((t != 6) & (t != 12) & (t != 18) & (r >= 6))
    source = jnp.where(is_rest, STACK * jnp.where(rest >= 3, 7, 6) + rest_row, source)
    source = source + HELD * (QUAD - 1 - owner)
    tally = ((t == 6) & (r < 2)) | ((t == 12) & (r >= 2) & (r < 6)) | ((t == 18) & (r >= 6))
    blank = (r & 1) == 1
    column = iota((QUAD * LINES, LANES), 1)
    picks = []
    for spare, shift in ((STACK - 8, 0), (0, 8)):
        here = jnp.where(tally, jnp.where(blank, -1, spare), source + shift)
        picks.append(
            jnp.concatenate([as_bf16(here == column), as_bf16(here == column + LANES)], axis=1)
        )
    ids_copy.wait()
    expert = iota((LANES, TOK), 0)
    named = jnp.zeros((LANES, TOK), jnp.float32)
    for k in range(TOP):
        named = named + (ids_ref[k : k + 1, :] == expert).astype(jnp.float32)
    counts = lax.dot_general(
        jnp.ones((16, TOK), jnp.bfloat16),
        named.astype(jnp.bfloat16),
        (((1,), (1,)), ((), ())),
        preferred_element_type=jnp.float32,
    )
    counts = jnp.concatenate([counts, counts], axis=1)
    upper = iota((16, 2 * LANES), 0) < 8
    for g in range(steps):
        if g in x_copies:
            x_copies[g].wait()
        one = x_ref[pl.ds(g * rows, rows // 2), :]
        two = x_ref[pl.ds(g * rows + rows // 2, rows // 2), :]
        thirds = []
        for i in range(8):
            here = slice(i * LANES, (i + 1) * LANES)
            both = jnp.concatenate([one[:, here], two[:, here]], axis=1)
            thirds.append((both[:16], both[16:32], both[32:]))
        middle = thirds[0][1].astype(jnp.float32)
        spare = (
            jnp.where(upper, middle, counts).astype(jnp.bfloat16),
            jnp.where(upper, counts, middle).astype(jnp.bfloat16),
        )
        packed = []
        for half in range(2):
            stack = [thirds[0][0], spare[0]] if half == 0 else [spare[1], thirds[0][2]]
            for i in range(1, 8):
                stack += thirds[i][half : half + 2]
            packed.append(
                jnp.dot(
                    picks[half], jnp.concatenate(stack, axis=0), preferred_element_type=jnp.float32
                )
            )
        packed = jnp.concatenate(packed[::-1], axis=0).astype(jnp.bfloat16)
        start = (steps - 1 - g) * 2 * OCT * LINES
        out_ref[pl.ds(start + OCT * LINES, OCT * LINES), :] = packed[:, :LANES]
        out_ref[pl.ds(start, OCT * LINES), :] = packed[:, LANES:]
        out_copies[g].start(priority=g % 2)
    for copy in out_copies:
        copy.wait()


def weights_kernel(ids_ref, route_ref, out_ref, odd_ref):
    expert = iota((EXPERTS, TOK), 0)
    named = jnp.zeros((EXPERTS, TOK), jnp.float32)
    weight = jnp.zeros((EXPERTS, TOK), jnp.float32)
    for k in range(TOP):
        hit = ids_ref[k : k + 1, :] == expert
        named = jnp.where(hit, 1.0, named)
        weight = jnp.where(hit, route_ref[k : k + 1, :], weight)
    before = as_bf16(iota((TOK, TOK), 0) < iota((TOK, TOK), 1))
    slot = jnp.dot(named.astype(jnp.bfloat16), before, preferred_element_type=jnp.float32)
    slot = jnp.where(named > 0, slot, -1.0)
    high = weight.astype(jnp.bfloat16)
    low = (weight - high.astype(jnp.float32)).astype(jnp.bfloat16)
    width = 8 * PEERS
    per_block = width // QUAD

    def holder_of(line):
        return PEERS - 1 - (QUAD * ((line % per_block) // 8) + line // per_block)

    spread = as_bf16(
        holder_of(iota((EXPERTS, width), 1)) // 2 == iota((EXPERTS, width), 0)
    )

    def over_lines(table):
        return lax.dot_general(
            table, spread, (((0,), (0,)), ((), ())), preferred_element_type=jnp.float32
        )

    slots = over_lines(slot.astype(jnp.bfloat16))
    highs, lows = over_lines(high), over_lines(low)
    line = iota((TOK, width), 1)
    q, r = line // per_block, line % 8
    first = HELD * (holder_of(line) % 2)
    slots = slots - first.astype(jnp.float32)

    def hits(wanted):
        return (slots == wanted.astype(jnp.float32)) & (wanted >= 0)

    main = jnp.where(r < HELD, r, -1)
    rests = [jnp.where(r < HELD, -1, 2 * i + r - HELD) for i in range(3)]
    for j, wanted in enumerate([main] + rests):
        hit = hits(wanted)
        for i, part in enumerate((highs, lows)):
            out_ref[j, i * TOK : (i + 1) * TOK, :] = jnp.where(hit, part, 0.0).astype(jnp.bfloat16)
    odd = hits(jnp.where(q == 1, r - 2, -1))
    shared = hits(
        jnp.where((q == 1) & (r < 2), r, jnp.where((q == 2) & (r >= 6), r - 2, -1))
    )
    wanted = ((odd, 1, highs), (odd, 1, lows))
    wanted += ((shared, 1, highs), (shared, 1, lows), (shared, 2, highs), (shared, 2, lows))
    for i, (hit, b, part) in enumerate(wanted):
        odd_ref[i * TOK : (i + 1) * TOK, :] = jnp.where(hit, part, 0.0)[
            :, b * per_block : (b + 1) * per_block
        ].astype(jnp.bfloat16)


def combine_kernel(weights_ref, odd_ref, arrived_ref, residual_ref, out_ref, load_ref):
    quads = PEERS // QUAD
    per_block = 8 * quads

    def tile(t):
        return arrived_ref[:, t].reshape(8 * quads, LANES)

    def columns(c):
        return slice(c * LANES, (c + 1) * LANES)

    r = iota((8, 8 * quads), 1) % 8
    load = jnp.zeros((8, LANES), jnp.float32)
    for t, wanted in ((6, r == 0), (12, (r == 2) | (r == 4)), (18, r == 6)):
        load = load + jnp.dot(as_bf16(wanted), tile(t), preferred_element_type=jnp.float32)
    load_ref[...] = load[:1, :EXPERTS]
    sums = jnp.dot(odd_ref[2 * TOK :], tile(12), preferred_element_type=jnp.float32)
    tails = [
        residual_ref[:, columns(6 + i)].astype(jnp.float32)
        + (sums[2 * i * TOK : (2 * i + 1) * TOK] + sums[(2 * i + 1) * TOK : (2 * i + 2) * TOK])
        for i in range(2)
    ]
    none = jnp.zeros((per_block, LANES), jnp.bfloat16)
    odd = {
        0: jnp.dot(odd_ref[: 2 * TOK], tile(6), preferred_element_type=jnp.float32),
        5: jnp.dot(
            weights_ref[0, :, 2 * per_block : 3 * per_block],
            tile(18),
            preferred_element_type=jnp.float32,
        ),
    }
    for c in range(3):
        lines = jnp.concatenate(
            [
                jnp.concatenate(
                    [none if f + i in (6, 18) else tile(f + i) for i in (c, c + 3)], axis=1
                )
                for f in FIRST
            ],
            axis=0,
        )
        sums = jnp.dot(
            jnp.concatenate([weights_ref[0], weights_ref[1 + c]], axis=0),
            lines,
            preferred_element_type=jnp.float32,
        )
        for i in range(2):
            part = sums[:, columns(i)]
            main = part[:TOK] + part[TOK : 2 * TOK]
            if c + 3 * i in odd:
                main = main + (odd[c + 3 * i][:TOK] + odd[c + 3 * i][TOK:])
            here = columns(c + 3 * i)
            out_ref[:, here] = (residual_ref[:, here].astype(jnp.float32) + main).astype(
                jnp.bfloat16
            )
            tails[i] = tails[i] + (part[2 * TOK : 3 * TOK] + part[3 * TOK :])
    for i in range(2):
        out_ref[:, columns(6 + i)] = tails[i].astype(jnp.bfloat16)


def per_device(residual, expert_ids, route_weights, expert_out):
    width = expert_out.shape[1]
    ids, routes = expert_ids.T, route_weights.T
    in_vmem = pl.BlockSpec(memory_space=pltpu.VMEM)
    in_hbm = pl.BlockSpec(memory_space=pltpu.HBM)
    steps = PEERS // (2 * OCT)
    packed = pl.pallas_call(
        pack_kernel,
        out_shape=jax.ShapeDtypeStruct((PEERS * LINES, LANES), jnp.bfloat16),
        in_specs=[in_hbm, in_hbm],
        out_specs=in_hbm,
        scratch_shapes=[
            pltpu.VMEM(expert_out.shape, jnp.bfloat16),
            pltpu.VMEM(ids.shape, jnp.int32),
            pltpu.VMEM((PEERS * LINES, LANES), jnp.bfloat16),
            pltpu.SemaphoreType.DMA((2,)),
            pltpu.SemaphoreType.DMA,
            pltpu.SemaphoreType.DMA((steps,)),
        ],
        compiler_params=pltpu.CompilerParams(vmem_limit_bytes=60 * 2**20),
        name="pack",
    )(expert_out, ids)
    arrived = lax.all_to_all(
        packed.reshape(PEERS, LINES // 2, 2, LANES),
        "expert",
        split_axis=0,
        concat_axis=0,
        axis_index_groups=[list(range(PEERS - 1, -1, -1))],
        tiled=True,
    ).reshape(PEERS // QUAD, TILES, 8, LANES)
    weights, odd = pl.pallas_call(
        weights_kernel,
        out_shape=(
            jax.ShapeDtypeStruct((4, 2 * TOK, 8 * PEERS), jnp.bfloat16),
            jax.ShapeDtypeStruct((6 * TOK, 8 * PEERS // QUAD), jnp.bfloat16),
        ),
        in_specs=[in_vmem, in_vmem],
        out_specs=(in_vmem, in_vmem),
        compiler_params=pltpu.CompilerParams(vmem_limit_bytes=24 * 2**20),
        name="weights",
    )(ids, routes)
    mixed, load = pl.pallas_call(
        combine_kernel,
        out_shape=(
            jax.ShapeDtypeStruct((TOK, width), jnp.bfloat16),
            jax.ShapeDtypeStruct((1, EXPERTS), jnp.float32),
        ),
        in_specs=[in_vmem, in_vmem, in_vmem, in_vmem],
        out_specs=(in_vmem, in_vmem),
        compiler_params=pltpu.CompilerParams(vmem_limit_bytes=24 * 2**20),
        name="combine",
    )(weights, odd, arrived, residual)
    return mixed, load.reshape(EXPERTS)


def solution(mesh):
    placed = P(("dp", "expert"), None)
    return jax.shard_map(
        per_device,
        mesh=mesh,
        in_specs=(placed, placed, placed, placed),
        out_specs=(placed, P("dp")),
        check_vma=False,
    )
```
